128 devices in a mesh: grp: 8 (over z_lo, y), blk: 16 (over x, z_hi, core).
Axes of the slice: x: 4, y: 4, z: 4 (z_hi: 2, z_lo: 2; z = z_hi * 2 + z_lo), core: 2. Of those that a mesh axis runs over, the one named last changes fastest.
Arguments:
- image_emb: bfloat16 [22528, 1152], P(('grp', 'blk')), may hold values from -16 to 16
- text_emb: bfloat16 [22528, 1152], P(('grp', 'blk')), may hold values from -16 to 16
- pair_ids: int32 [22528], P(('grp', 'blk')), may hold values from 0 to 703
- logit_scale: float32 [1], replicated, may hold values from 2.3 to 2.8
- bias: float32 [1], replicated, may hold values from -2.5 to -0.5
Outputs:
- image_grad: bfloat16 [22528, 1152], P(('grp', 'blk'))
- text_grad: bfloat16 [22528, 1152], P(('grp', 'blk'))
The draws below stay inside these ranges and needn't reach their ends.
All inputs are finite; a program needn't handle non-finite values.
Results may differ from the reference program's by a relative error of at most 0.019.
Values may be sent and summed in bfloat16 or wider, within the bound.
A program may use at most 128 MiB of HBM per device.

```python
import math
import jax
import jax.numpy as jnp
from jax import lax

D = 1152
ROWS_DEV = 176
TOKENS = 22528
N_GRP = 8


def shared_centers(key, cluster_count):
    centers = jax.random.normal(key, (cluster_count, D), jnp.float32)
    return jnp.clip(centers, -5.0, 5.0) / math.sqrt(D)


def clustered_base(key, centers, lowest, highest, cluster_count):
    key_choose, key_strength = jax.random.split(key, 2)
    chosen = jax.random.randint(key_choose, (TOKENS,), 0, cluster_count)
    strength = jax.random.uniform(key_strength, (TOKENS, 1), jnp.float32, lowest, highest)
    return strength * centers[chosen]


def normal_jitter(key):
    jitter = jax.random.normal(key, (TOKENS, D), jnp.float32)
    return jnp.clip(jitter, -5.0, 5.0) / math.sqrt(D)


def draw_image_emb(key, part):
    centers = shared_centers(key, 24)
    key = jax.random.fold_in(key, 11)
    key_base, key_jitter = jax.random.split(key, 2)
    values = clustered_base(key_base, centers, 0.3, 1.5, 24) + normal_jitter(key_jitter)
    return values.astype(jnp.bfloat16)


def draw_text_emb(key, part):
    centers = shared_centers(key, 24)
    key = jax.random.fold_in(key, 23)
    key_base, key_jitter = jax.random.split(key, 2)
    values = clustered_base(key_base, centers, 0.3, 1.5, 24) + normal_jitter(key_jitter)
    return values.astype(jnp.bfloat16)


def plant(values, rng, smallest, largest):
    longest = values.shape.index(max(values.shape))
    spots = []
    for shift in (0, 1):
        where = [jax.random.randint(jax.random.fold_in(rng, axis), (), 0, length) for axis, length in enumerate(values.shape)]
        where[longest] = (where[longest] + shift) % values.shape[longest]
        spots.append(tuple(where))
    return values.at[spots[0]].set(smallest).at[spots[1]].set(largest)


def setup_inputs(seed: int = 0) -> dict:
    arg_keys = jax.random.split(jax.random.key(seed), 6)
    image_emb = draw_image_emb(jax.random.fold_in(arg_keys[5], 71), 0)
    text_emb = draw_text_emb(jax.random.fold_in(arg_keys[5], 71), 0)
    pair_ids = plant(jax.random.randint(arg_keys[2], (TOKENS,), 0, TOKENS // 32), jax.random.fold_in(arg_keys[2], 1), 0, (TOKENS // 32) - 1).astype(jnp.int32)
    logit_scale = jnp.clip(jax.random.uniform(arg_keys[3], (1,), jnp.float32, 2.3, 2.8), 2.3, 2.8)
    bias = jnp.clip(jax.random.uniform(arg_keys[4], (1,), jnp.float32, -2.5, -0.5), -2.5, -0.5)
    return dict(image_emb=image_emb, text_emb=text_emb, pair_ids=pair_ids, logit_scale=logit_scale, bias=bias)


epsilon = 1e-06

def unit_rows(embedding):
    values = embedding.astype(jnp.float32)
    inverse = lax.rsqrt(lax.optimization_barrier(jnp.sum(values * values, axis=1, keepdims=True)) + epsilon)
    return (values * inverse, inverse)

def finish(scaled, inverse, gradient):
    along = lax.optimization_barrier(jnp.sum(scaled * gradient, axis=1, keepdims=True))
    return ((gradient - scaled * along) * inverse).astype(jnp.bfloat16)

def factor_block(texts, text_ids, images, image_ids, scale, offset):
    products = lax.dot_general(texts, images, (((1,), (1,)), ((), ())), preferred_element_type=jnp.float32)
    logits = scale * products + offset
    signs = jnp.where(text_ids[:, None] == image_ids[None, :], jnp.float32(1.0), jnp.float32(-1.0))
    return (-signs * jax.nn.sigmoid(-signs * logits) * scale).astype(jnp.bfloat16)

def reference(image_emb, text_emb, pair_ids, logit_scale, bias):
    image_scaled, image_inverse = unit_rows(image_emb)
    text_scaled, text_inverse = unit_rows(text_emb)
    image_unit = image_scaled.astype(jnp.bfloat16)
    text_unit = text_scaled.astype(jnp.bfloat16)
    scale = jnp.exp(logit_scale[0])
    offset = bias[0]
    block_rows = ROWS_DEV * N_GRP
    blocks = TOKENS // block_rows
    text_blocks = text_unit.reshape(blocks, block_rows, D)
    id_blocks = pair_ids.reshape(blocks, block_rows)

    def visit(image_total, pieces):
        texts, text_ids = pieces
        factors = factor_block(texts, text_ids, image_unit, pair_ids, scale, offset)
        image_total = image_total + lax.dot_general(factors, texts, (((0,), (0,)), ((), ())), preferred_element_type=jnp.float32)
        text_part = jnp.dot(factors, image_unit, preferred_element_type=jnp.float32)
        return (image_total, text_part)
    image_total, text_parts = lax.scan(visit, jnp.zeros((TOKENS, D), jnp.float32), (text_blocks, id_blocks))
    text_total = text_parts.reshape(TOKENS, D)
    return (finish(image_scaled, image_inverse, image_total), finish(text_scaled, text_inverse, text_total))
```

```python
import functools
import math

import jax
import jax.numpy as jnp
from jax import lax
from jax.experimental import pallas as pl
from jax.experimental.pallas import tpu as pltpu
from jax.sharding import PartitionSpec as P

epsilon = 1e-06
MESH = pl.DeviceIdType.MESH
NT = (((1,), (1,)), ((), ()))
TN = (((0,), (0,)), ((), ()))
LOG2E = math.log2(math.e)


def places():
    g, b = lax.axis_index("grp"), lax.axis_index("blk")
    z_lo, y = g // 4, g % 4
    x, z_hi, core = b // 4, (b // 2) % 2, b % 2
    z = z_hi * 2 + z_lo

    def device(x, y, z, core):
        return ((z % 2) * 4 + y, x * 4 + (z // 2) * 2 + core)

    toward_a, toward_b = 3 - 2 * core, 1 + 2 * core
    text = dict(
        a=device((x + toward_a) % 4, y, z, core),
        b=device((x + toward_b) % 4, y, z, core),
        z=device(x, y, (z // 2) * 2 + 1 - z % 2, core),
    )
    image = dict(
        a=device(x, (y + toward_a) % 4, z, core),
        b=device(x, (y + toward_b) % 4, z, core),
        z=device(x, y, 3 - z, core),
    )
    return text, image, device(x, y, z, 1 - core), core


def unit_rows(embedding):
    values = embedding.astype(jnp.float32)
    inverse = lax.rsqrt(jnp.sum(values * values, axis=1, keepdims=True) + epsilon)
    return values * inverse, inverse


def kernel(rows, width, image_in, text_in, ids_in, scale_in, bias_in, image_out, text_out,
           texts, images, text_ids, image_ids, text_col, image_col, image_row, factors, text_acc, image_acc,
           sib_out, sib_in, text_send, text_recv, image_send, image_recv,
           gt_s, gt_r, gi_s, gi_r, gs_s, gs_r, ht_s, ht_r, hi_s, hi_r, hs_s, hs_r,
           rt_s, rt_r, ri_s, ri_r, rs_s, rs_r):
    pair = 2 * rows
    text_at, image_at, sibling, core = places()
    near_a, near_b, far_a, far_b = 3 - core, 2 + core, 6 - core, 5 + core

    barrier = pltpu.get_barrier_semaphore()
    partners = [*text_at.values(), *image_at.values(), sibling]
    for partner in partners:
        pl.semaphore_signal(barrier, inc=1, device_id=partner, device_id_type=MESH)

    scale = jnp.exp(scale_in[0])
    scale2, offset2 = scale * LOG2E, bias_in[0] * LOG2E

    def text_rows(k):
        return pl.ds(pl.multiple_of(k * pair, 16), rows)

    def sib_rows(k):
        return pl.ds(pl.multiple_of(k * pair + rows, 16), rows)

    def image_rows(k):
        return pl.ds(pl.multiple_of(k * rows, 16), rows)

    texts[text_rows(0), :] = unit_rows(text_in[...])[0].astype(jnp.bfloat16)
    images[image_rows(0), :] = unit_rows(image_in[...])[0].astype(jnp.bfloat16)
    own_ids = jnp.broadcast_to(ids_in[...], (8, 256))
    text_ids[0] = own_ids
    image_ids[0] = own_ids
    pl.semaphore_wait(barrier, len(partners))

    sent = []

    def remote(src, dst, send, recv, to):
        return pltpu.make_async_remote_copy(
            src_ref=src, dst_ref=dst, send_sem=send, recv_sem=recv, device_id=to, device_id_type=MESH
        )

    def launch(copy):
        copy.start()
        sent.append(copy)

    def push_text(message, k, k_there, to):
        launch(remote(texts.at[text_rows(k), :], texts.at[text_rows(k_there), :], gt_s.at[message], gt_r.at[message], to))
        launch(remote(text_ids.at[2 * k], text_ids.at[2 * k_there], ht_s.at[message], ht_r.at[message], to))

    def push_image(message, k, k_there, to):
        launch(remote(images.at[image_rows(k), :], images.at[image_rows(k_there), :], gi_s.at[message], gi_r.at[message], to))
        launch(remote(image_ids.at[k], image_ids.at[k_there], hi_s.at[message], hi_r.at[message], to))

    def push_sibling(k):
        launch(remote(texts.at[text_rows(k), :], texts.at[sib_rows(k), :], gs_s.at[k], gs_r.at[k], sibling))
        launch(remote(text_ids.at[2 * k], text_ids.at[2 * k + 1], hs_s.at[k], hs_r.at[k], sibling))

    def took_text(message, k):
        place = texts.at[text_rows(k), :]
        remote(place, place, gt_s.at[message], gt_r.at[message], sibling).wait_recv()
        place = text_ids.at[2 * k]
        remote(place, place, ht_s.at[message], ht_r.at[message], sibling).wait_recv()

    def took_image(message, k):
        place = images.at[image_rows(k), :]
        remote(place, place, gi_s.at[message], gi_r.at[message], sibling).wait_recv()
        place = image_ids.at[k]
        remote(place, place, hi_s.at[message], hi_r.at[message], sibling).wait_recv()

    def took_sibling(k):
        place = texts.at[sib_rows(k), :]
        remote(place, place, gs_s.at[k], gs_r.at[k], sibling).wait_recv()
        place = text_ids.at[2 * k + 1]
        remote(place, place, hs_s.at[k], hs_r.at[k], sibling).wait_recv()

    def column(ids):
        return jnp.transpose(ids)[:rows, 0:1]

    def text_columns(blocks):
        for k in blocks:
            text_col[k * pair:k * pair + rows, :] = column(text_ids[2 * k])
            text_col[k * pair + rows:(k + 1) * pair, :] = column(text_ids[2 * k + 1])

    def image_columns(blocks):
        for k in blocks:
            image_col[k * rows:(k + 1) * rows, :] = column(image_ids[k])

    def image_window(first, last):
        for w in range(first, last, 128):
            image_row[:, w:w + 128] = jnp.transpose(jnp.broadcast_to(image_col[w:w + 128, :], (128, 128)))[0:8, :]

    def factor_strip(start, count, first, last):
        some = pl.ds(start, count)
        products = lax.dot_general(texts[some, :], images[first:last, :], NT, preferred_element_type=jnp.float32)
        e = jnp.exp2(products * scale2 + offset2)
        match = text_col[some, :] == image_row[0:1, first:last]
        factors[some, first:last] = (jnp.where(match, -1.0, e) / (1.0 + e)).astype(jnp.bfloat16)

    def factor_block(start, blocks, first, last):
        def strip(n, carry):
            factor_strip(pl.multiple_of(start + n * pair, 16), pair, first, last)
            return carry

        lax.fori_loop(0, blocks, strip, 0)

    def text_gradient(k):
        part = jnp.dot(factors[pl.ds(pl.multiple_of(k * pair, 16), pair), :], images[...], preferred_element_type=jnp.float32)
        text_acc[image_rows(k), :] = part[:rows]
        sib_out[k] = part[rows:].astype(jnp.bfloat16)
        launch(remote(sib_out.at[k], sib_in.at[k], rs_s.at[k], rs_r.at[k], sibling))

    def image_gradient(first, last):
        image_acc[first:last, :] = lax.dot_general(
            factors[:, first:last], texts[...], TN, preferred_element_type=jnp.float32)

    def landed(buffer, sends, recvs, message):
        remote(buffer.at[message], buffer.at[message], sends.at[message], recvs.at[message], sibling).wait_recv()
        return buffer[message].astype(jnp.float32)

    def text_sum(k, messages):
        remote(sib_in.at[k], sib_in.at[k], rs_s.at[k], rs_r.at[k], sibling).wait_recv()
        total = text_acc[image_rows(k), :] + sib_in[k].astype(jnp.float32)
        for message in messages:
            total = total + landed(text_recv, rt_s, rt_r, message)
        return total

    def image_sum(k, messages):
        total = image_acc[image_rows(k), :]
        for message in messages:
            total = total + landed(image_recv, ri_s, ri_r, message)
        return total

    def text_hop(k, messages, message, to):
        text_send[message] = text_sum(k, messages).astype(jnp.bfloat16)
        launch(remote(text_send.at[message], text_recv.at[message], rt_s.at[message], rt_r.at[message], to))

    def image_hop(k, messages, message, to):
        image_send[message] = image_sum(k, messages).astype(jnp.bfloat16)
        launch(remote(image_send.at[message], image_recv.at[message], ri_s.at[message], ri_r.at[message], to))

    def finish(embedding, gradient):
        scaled, inverse = unit_rows(embedding)
        gradient = gradient * scale
        along = jnp.sum(scaled * gradient, axis=1, keepdims=True)
        return ((gradient - scaled * along) * inverse).astype(jnp.bfloat16)

    push_text(1, 0, near_a, text_at["b"])
    push_image(1, 0, near_a, image_at["b"])
    push_text(0, 0, near_b, text_at["a"])
    push_image(0, 0, near_b, image_at["a"])
    push_text(2, 0, 1, text_at["z"])
    push_image(2, 0, 1, image_at["z"])
    push_sibling(0)

    took_text(1, near_a)
    push_text(3, near_a, 4, text_at["b"])
    took_image(1, near_a)
    push_image(3, near_a, 4, image_at["b"])
    took_text(2, 1)
    push_text(4, 1, far_b, text_at["a"])
    push_text(5, 1, far_a, text_at["b"])
    took_image(2, 1)
    push_image(4, 1, far_b, image_at["a"])
    push_image(5, 1, far_a, image_at["b"])
    push_sibling(near_a)
    push_sibling(1)
    took_text(0, near_b)
    push_sibling(near_b)
    took_image(0, near_b)
    image_columns([0, 1, 2, 3])
    image_window(0, 512)
    for k in (0, near_a, 1, near_b):
        took_sibling(k)
    text_columns([0, 1, 2, 3])
    factor_block(0, 4, 0, 512)

    took_text(3, 4)
    push_text(6, 4, 7, text_at["z"])
    took_image(3, 4)
    push_image(6, 4, 7, image_at["z"])
    push_sibling(4)
    image_columns([4])
    image_window(512, 768)
    took_sibling(4)
    text_columns([4])
    factor_block(0, 4, 512, 768)
    factor_block(4 * pair, 1, 0, 768)

    took_text(4, far_b)
    push_sibling(far_b)
    took_text(5, far_a)
    push_sibling(far_a)
    took_text(6, 7)
    push_sibling(7)
    took_image(4, far_b)
    took_image(5, far_a)
    took_image(6, 7)
    image_columns([5, 6, 7])
    image_window(768, 1408)
    for k in (far_b, far_a, 7):
        took_sibling(k)
    text_columns([5, 6, 7])

    factor_block(7 * pair, 1, 0, 1408)
    text_gradient(7)
    factor_block(5 * pair, 2, 0, 1408)
    text_hop(7, (), 0, text_at["z"])
    text_gradient(far_a)
    text_gradient(far_b)
    factor_block(0, 2, 768, 1408)
    text_hop(far_a, (), 2, text_at["a"])
    text_hop(far_b, (), 3, text_at["b"])
    factor_block(2 * pair, 3, 768, 1408)
    image_gradient(1152, 1408)
    image_hop(7, (), 0, image_at["z"])
    image_gradient(768, 1152)
    image_hop(far_a, (), 2, image_at["a"])
    image_hop(far_b, (), 3, image_at["b"])
    text_gradient(4)
    image_gradient(640, 768)
    text_hop(4, (0,), 1, text_at["a"])
    text_gradient(1)
    image_hop(4, (0,), 1, image_at["a"])
    text_gradient(near_b)
    text_gradient(near_a)
    text_hop(near_b, (), 5, text_at["b"])
    text_hop(1, (2, 3), 6, text_at["z"])
    image_gradient(384, 640)
    image_gradient(128, 384)
    text_hop(near_a, (1,), 4, text_at["a"])
    image_hop(near_b, (), 5, image_at["b"])
    image_hop(1, (2, 3), 6, image_at["z"])
    image_gradient(0, 128)
    text_gradient(0)
    image_hop(near_a, (1,), 4, image_at["a"])
    text_out[...] = finish(text_in[...], text_sum(0, (5, 6, 4)))
    image_out[...] = finish(image_in[...], image_sum(0, (5, 6, 4)))
    for copy in sent:
        copy.wait_send()


def local(image_emb, text_emb, pair_ids, logit_scale, bias):
    rows, width = image_emb.shape
    ids = jnp.pad(pair_ids, (0, 256 - rows)).reshape(1, 256)
    bf16, f32, i32 = jnp.bfloat16, jnp.float32, jnp.int32
    vmem, smem = pl.BlockSpec(memory_space=pltpu.VMEM), pl.BlockSpec(memory_space=pltpu.SMEM)
    dma = pltpu.SemaphoreType.DMA
    return pl.pallas_call(
        functools.partial(kernel, rows, width),
        out_shape=[jax.ShapeDtypeStruct((rows, width), bf16)] * 2,
        in_specs=[vmem, vmem, vmem, smem, smem],
        out_specs=[vmem, vmem],
        scratch_shapes=[
            pltpu.VMEM((16 * rows, width), bf16),
            pltpu.VMEM((8 * rows, width), bf16),
            pltpu.VMEM((16, 8, 256), i32),
            pltpu.VMEM((8, 8, 256), i32),
            pltpu.VMEM((16 * rows, 1), i32),
            pltpu.VMEM((8 * rows, 1), i32),
            pltpu.VMEM((8, 8 * rows), i32),
            pltpu.VMEM((16 * rows, 8 * rows), bf16),
            pltpu.VMEM((8 * rows, width), f32),
            pltpu.VMEM((8 * rows, width), f32),
            pltpu.VMEM((8, rows, width), bf16),
            pltpu.VMEM((8, rows, width), bf16),
            pltpu.VMEM((7, rows, width), bf16),
            pltpu.VMEM((7, rows, width), bf16),
            pltpu.VMEM((7, rows, width), bf16),
            pltpu.VMEM((7, rows, width), bf16),
        ]
        + [dma((7,))] * 4 + [dma((8,))] * 2 + [dma((7,))] * 4 + [dma((8,))] * 2
        + [dma((7,))] * 4 + [dma((8,))] * 2,
        compiler_params=pltpu.CompilerParams(
            collective_id=0, has_side_effects=True, vmem_limit_bytes=63 << 20
        ),
    )(image_emb, text_emb, ids, logit_scale, bias)


def solution(mesh):
    placed = (P(("grp", "blk"), None), P(("grp", "blk"), None), P(("grp", "blk")), P(), P())
    return jax.shard_map(
        local,
        mesh=mesh,
        in_specs=placed,
        out_specs=(P(("grp", "blk"), None), P(("grp", "blk"), None)),
        check_vma=False,
    )
```

```python
import functools
import math

import jax
import jax.numpy as jnp
from jax import lax
from jax.experimental import pallas as pl
from jax.experimental.pallas import tpu as pltpu
from jax.sharding import PartitionSpec as P

epsilon = 1e-06
MESH = pl.DeviceIdType.MESH
NT = (((1,), (1,)), ((), ()))
TN = (((0,), (0,)), ((), ()))
LOG2E = math.log2(math.e)


def places():
    g, b = lax.axis_index("grp"), lax.axis_index("blk")
    z_lo, y = g // 4, g % 4
    x, z_hi, core = b // 4, (b // 2) % 2, b % 2
    z = z_hi * 2 + z_lo

    def device(x, y, z, core):
        return ((z % 2) * 4 + y, x * 4 + (z // 2) * 2 + core)

    toward_a, toward_b = 3 - 2 * core, 1 + 2 * core
    text = dict(
        a=device((x + toward_a) % 4, y, z, core),
        b=device((x + toward_b) % 4, y, z, core),
        z=device(x, y, (z // 2) * 2 + 1 - z % 2, core),
    )
    image = dict(
        a=device(x, (y + toward_a) % 4, z, core),
        b=device(x, (y + toward_b) % 4, z, core),
        z=device(x, y, 3 - z, core),
    )
    return text, image, device(x, y, z, 1 - core), core


def unit_rows(embedding):
    values = embedding.astype(jnp.float32)
    inverse = lax.rsqrt(jnp.sum(values * values, axis=1, keepdims=True) + epsilon)
    return values * inverse, inverse


def kernel(rows, width, image_in, text_in, ids_in, scale_in, bias_in, image_out, text_out,
           texts, images, text_ids, image_ids, text_col, image_col, image_row, factors, text_acc, text_far, image_acc,
           sib_out, sib_in, text_send, text_recv, image_send, image_recv,
           gt_s, gt_r, gi_s, gi_r, gs_s, gs_r, ht_s, ht_r, hi_s, hi_r, hs_s, hs_r,
           rt_s, rt_r, ri_s, ri_r, rs_s, rs_r):
    pair = 2 * rows
    text_at, image_at, sibling, core = places()
    near_a, near_b, far_a, far_b = 3 - core, 2 + core, 6 - core, 5 + core

    barrier = pltpu.get_barrier_semaphore()
    partners = [*text_at.values(), *image_at.values(), sibling]
    for partner in partners:
        pl.semaphore_signal(barrier, inc=1, device_id=partner, device_id_type=MESH)

    scale = jnp.exp(scale_in[0])
    scale2, offset2 = scale * LOG2E, bias_in[0] * LOG2E

    def text_rows(k):
        return pl.ds(pl.multiple_of(k * pair, 16), rows)

    def sib_rows(k):
        return pl.ds(pl.multiple_of(k * pair + rows, 16), rows)

    def image_rows(k):
        return pl.ds(pl.multiple_of(k * rows, 16), rows)

    texts[text_rows(0), :] = unit_rows(text_in[...])[0].astype(jnp.bfloat16)
    images[image_rows(0), :] = unit_rows(image_in[...])[0].astype(jnp.bfloat16)
    for held in (text_ids, image_ids):
        held[0] = jnp.zeros((8, 256), jnp.int32)
        held[0, :, 0:rows] = jnp.broadcast_to(ids_in[...], (8, rows))
    pl.semaphore_wait(barrier, len(partners))

    sent = []

    def remote(src, dst, send, recv, to):
        return pltpu.make_async_remote_copy(
            src_ref=src, dst_ref=dst, send_sem=send, recv_sem=recv, device_id=to, device_id_type=MESH
        )

    def launch(copy):
        copy.start()
        sent.append(copy)

    def push_text(message, k, k_there, to, ids=True):
        launch(remote(texts.at[text_rows(k), :], texts.at[text_rows(k_there), :], gt_s.at[message], gt_r.at[message], to))
        if ids:
            launch(remote(text_ids.at[2 * k], text_ids.at[2 * k_there], ht_s.at[message], ht_r.at[message], to))

    def push_image(message, k, k_there, to, ids=True):
        launch(remote(images.at[image_rows(k), :], images.at[image_rows(k_there), :], gi_s.at[message], gi_r.at[message], to))
        if ids:
            launch(remote(image_ids.at[k], image_ids.at[k_there], hi_s.at[message], hi_r.at[message], to))

    def push_sibling(k):
        launch(remote(texts.at[text_rows(k), :], texts.at[sib_rows(k), :], gs_s.at[k], gs_r.at[k], sibling))
        launch(remote(text_ids.at[2 * k], text_ids.at[2 * k + 1], hs_s.at[k], hs_r.at[k], sibling))

    def took_text(message, k):
        place = texts.at[text_rows(k), :]
        remote(place, place, gt_s.at[message], gt_r.at[message], sibling).wait_recv()
        place = text_ids.at[2 * k]
        remote(place, place, ht_s.at[message], ht_r.at[message], sibling).wait_recv()

    def took_image(message, k):
        place = images.at[image_rows(k), :]
        remote(place, place, gi_s.at[message], gi_r.at[message], sibling).wait_recv()
        place = image_ids.at[k]
        remote(place, place, hi_s.at[message], hi_r.at[message], sibling).wait_recv()

    def took_sibling(k):
        place = texts.at[sib_rows(k), :]
        remote(place, place, gs_s.at[k], gs_r.at[k], sibling).wait_recv()
        place = text_ids.at[2 * k + 1]
        remote(place, place, hs_s.at[k], hs_r.at[k], sibling).wait_recv()

    def column(ids):
        return jnp.transpose(ids)[:rows, 0:1]

    def text_columns(blocks):
        for k in blocks:
            text_col[k * pair:k * pair + rows, :] = column(text_ids[2 * k])
            text_col[k * pair + rows:(k + 1) * pair, :] = column(text_ids[2 * k + 1])

    def image_columns(blocks):
        for k in blocks:
            image_col[k * rows:(k + 1) * rows, :] = column(image_ids[k])

    def image_window(first, last):
        for w in range(first, last, 128):
            image_row[:, w:w + 128] = jnp.transpose(jnp.broadcast_to(image_col[w:w + 128, :], (128, 128)))[0:8, :]

    def factor_strip(start, count, first, last):
        some = pl.ds(start, count)
        products = lax.dot_general(texts[some, :], images[first:last, :], NT, preferred_element_type=jnp.float32)
        e = jnp.exp2(products * scale2 + offset2)
        match = text_col[some, :] == image_row[0:1, first:last]
        factors[some, first:last] = (jnp.where(match, -1.0, e) * pltpu.reciprocal(1.0 + e, approx=True)).astype(jnp.bfloat16)

    def factor_block(start, blocks, first, last):
        def strip(n, carry):
            factor_strip(pl.multiple_of(start + n * pair, 16), pair, first, last)
            return carry

        lax.fori_loop(0, blocks, strip, 0)

    near_texts, near_images = 5 * pair, 768

    def text_pairs(k):
        return pl.ds(pl.multiple_of(k * pair, 16), pair)

    def to_sibling(k, part):
        sib_out[k] = part.astype(jnp.bfloat16)
        launch(remote(sib_out.at[k], sib_in.at[k], rs_s.at[k], rs_r.at[k], sibling))

    def early_text_gradients():
        def strip(k, carry):
            text_acc[text_pairs(k), :] = jnp.dot(
                factors[text_pairs(k), :near_images], images[:near_images, :], preferred_element_type=jnp.float32)
            return carry

        lax.fori_loop(0, 5, strip, 0)

    def text_gradient(k):
        part = jnp.dot(factors[text_pairs(k), near_images:], images[near_images:, :], preferred_element_type=jnp.float32)
        part = text_acc[text_pairs(k), :] + part
        text_acc[text_rows(k), :] = part[:rows]
        to_sibling(k, part[rows:])

    def far_text_gradient(k):
        part = jnp.dot(factors[text_pairs(k), :], images[...], preferred_element_type=jnp.float32)
        text_far[image_rows(k - 5), :] = part[:rows]
        to_sibling(k, part[rows:])

    def early_image_gradients(low, high):
        for first in range(low, high, 256):
            image_acc[first:first + 256, :] = lax.dot_general(
                factors[:near_texts, first:first + 256], texts[:near_texts, :], TN, preferred_element_type=jnp.float32)

    def image_gradient(first, last):
        image_acc[first:last, :] += lax.dot_general(
            factors[near_texts:, first:last], texts[near_texts:, :], TN, preferred_element_type=jnp.float32)

    def far_image_gradient(first, last):
        image_acc[first:last, :] = lax.dot_general(
            factors[:, first:last], texts[...], TN, preferred_element_type=jnp.float32)

    pieces = ((0, 96), (96, rows - 96))

    def piece_rows(start, p):
        return pl.ds(pl.multiple_of(start + pieces[p][0], 16), pieces[p][1])

    def wire(buffer, m, p):
        return buffer.at[m, pl.ds(*pieces[p]), :]

    def landed(buffer, sends, recvs, m, p):
        place = wire(buffer, m, p)
        remote(place, place, sends.at[p, m], recvs.at[p, m], sibling).wait_recv()
        return place[...].astype(jnp.float32)

    def text_sum(k, messages, p, far=False):
        if p == 0:
            remote(sib_in.at[k], sib_in.at[k], rs_s.at[k], rs_r.at[k], sibling).wait_recv()
        held = text_far[piece_rows((k - 5) * rows, p), :] if far else text_acc[piece_rows(k * pair, p), :]
        total = held + wire(sib_in, k, p)[...].astype(jnp.float32)
        for m in messages:
            total = total + landed(text_recv, rt_s, rt_r, m, p)
        return total

    def image_sum(k, messages, p):
        total = image_acc[piece_rows(k * rows, p), :]
        for m in messages:
            total = total + landed(image_recv, ri_s, ri_r, m, p)
        return total

    def text_hop(k, messages, m, to, far=False, some=(0, 1)):
        for p in some:
            wire(text_send, m, p)[...] = text_sum(k, messages, p, far).astype(jnp.bfloat16)
            launch(remote(wire(text_send, m, p), wire(text_recv, m, p), rt_s.at[p, m], rt_r.at[p, m], text_at[to]))

    def image_hop(k, messages, m, to, some=(0, 1)):
        for p in some:
            wire(image_send, m, p)[...] = image_sum(k, messages, p).astype(jnp.bfloat16)
            launch(remote(wire(image_send, m, p), wire(image_recv, m, p), ri_s.at[p, m], ri_r.at[p, m], image_at[to]))

    def finish(embedding, gradient):
        scaled, inverse = unit_rows(embedding)
        gradient = gradient * scale
        along = jnp.sum(scaled * gradient, axis=1, keepdims=True)
        return ((gradient - scaled * along) * inverse).astype(jnp.bfloat16)

    def text_done(p):
        some = pl.ds(*pieces[p])
        text_out[some, :] = finish(text_in[some, :], text_sum(0, (5, 6, 4), p))

    def image_done(p):
        some = pl.ds(*pieces[p])
        image_out[some, :] = finish(image_in[some, :], image_sum(0, (5, 6, 4), p))

    for m, k_there, to in ((1, near_a, "b"), (0, near_b, "a"), (2, 1, "z")):
        push_text(m, 0, k_there, text_at[to], False)
        push_image(m, 0, k_there, image_at[to], False)
    push_sibling(0)
    for m, k_there, to in ((1, near_a, "b"), (0, near_b, "a"), (2, 1, "z")):
        launch(remote(text_ids.at[0], text_ids.at[2 * k_there], ht_s.at[m], ht_r.at[m], text_at[to]))
        launch(remote(image_ids.at[0], image_ids.at[k_there], hi_s.at[m], hi_r.at[m], image_at[to]))

    took_text(1, near_a)
    push_text(3, near_a, 4, text_at["b"])
    took_image(1, near_a)
    push_image(3, near_a, 4, image_at["b"])
    took_text(2, 1)
    push_sibling(near_a)
    push_sibling(1)
    took_text(0, near_b)
    push_sibling(near_b)
    took_image(2, 1)
    took_image(0, near_b)
    image_columns([0, 1, 2, 3])
    image_window(0, 512)
    for k in (0, near_a, 1, near_b):
        took_sibling(k)
    text_columns([0, 1, 2, 3])
    factor_block(0, 4, 0, 512)

    took_text(3, 4)
    push_text(6, 4, 7, text_at["z"])
    push_text(4, 1, far_b, text_at["a"])
    push_text(5, 1, far_a, text_at["b"])
    took_image(3, 4)
    push_image(6, 4, 7, image_at["z"])
    push_image(4, 1, far_b, image_at["a"])
    push_image(5, 1, far_a, image_at["b"])
    push_sibling(4)
    image_columns([4])
    image_window(512, 768)
    took_sibling(4)
    text_columns([4])
    factor_block(0, 4, 512, 768)
    factor_block(4 * pair, 1, 0, 768)
    early_text_gradients()
    early_image_gradients(0, 512)

    took_text(4, far_b)
    push_sibling(far_b)
    took_text(5, far_a)
    push_sibling(far_a)
    took_text(6, 7)
    push_sibling(7)
    took_image(4, far_b)
    took_image(5, far_a)
    took_image(6, 7)
    early_image_gradients(512, 768)
    image_columns([5, 6, 7])
    image_window(768, 1408)
    for k in (far_b, far_a, 7):
        took_sibling(k)
    text_columns([5, 6, 7])

    factor_block(7 * pair, 1, 0, 1408)
    far_text_gradient(7)
    factor_block(5 * pair, 1, 0, 1408)
    text_hop(7, (), 0, "z", far=True)
    factor_block(6 * pair, 1, 0, 1408)
    image_gradient(256, 768)
    image_hop(near_b, (), 5, "b")
    far_text_gradient(5)
    far_text_gradient(6)
    factor_block(0, 2, 768, 1408)
    text_hop(far_a, (), 2, "a", far=True)
    text_hop(far_b, (), 3, "b", far=True)
    factor_block(2 * pair, 3, 768, 1408)
    far_image_gradient(1152, 1408)
    image_hop(7, (), 0, "z")
    far_image_gradient(768, 1152)
    image_hop(far_a, (), 2, "a")
    image_hop(far_b, (), 3, "b")
    text_gradient(4)
    text_gradient(2)
    text_hop(4, (0,), 1, "a")
    text_gradient(3)
    text_gradient(1)
    text_hop(near_b, (), 5, "b")
    image_gradient(0, 256)
    text_hop(1, (2, 3), 6, "z")
    image_hop(4, (0,), 1, "a", (0,))
    text_gradient(0)
    image_hop(4, (0,), 1, "a", (1,))
    image_hop(1, (2, 3), 6, "z", (0,))
    text_hop(near_a, (1,), 4, "a")
    image_hop(1, (2, 3), 6, "z", (1,))
    image_hop(near_a, (1,), 4, "a", (0,))
    image_hop(near_a, (1,), 4, "a", (1,))
    text_done(0)
    text_done(1)
    image_done(0)
    image_done(1)
    for copy in sent:
        copy.wait_send()


def local(image_emb, text_emb, pair_ids, logit_scale, bias):
    rows, width = image_emb.shape
    ids = pair_ids.reshape(1, rows)
    bf16, f32, i32 = jnp.bfloat16, jnp.float32, jnp.int32
    vmem, smem = pl.BlockSpec(memory_space=pltpu.VMEM), pl.BlockSpec(memory_space=pltpu.SMEM)
    dma = pltpu.SemaphoreType.DMA
    return pl.pallas_call(
        functools.partial(kernel, rows, width),
        out_shape=[jax.ShapeDtypeStruct((rows, width), bf16)] * 2,
        in_specs=[vmem, vmem, vmem, smem, smem],
        out_specs=[vmem, vmem],
        scratch_shapes=[
            pltpu.VMEM((16 * rows, width), bf16),
            pltpu.VMEM((8 * rows, width), bf16),
            pltpu.VMEM((16, 8, 256), i32),
            pltpu.VMEM((8, 8, 256), i32),
            pltpu.VMEM((16 * rows, 1), i32),
            pltpu.VMEM((8 * rows, 1), i32),
            pltpu.VMEM((8, 8 * rows), i32),
            pltpu.VMEM((16 * rows, 8 * rows), bf16),
            pltpu.VMEM((10 * rows, width), f32),
            pltpu.VMEM((3 * rows, width), f32),
            pltpu.VMEM((8 * rows, width), f32),
            pltpu.VMEM((8, rows, width), bf16),
            pltpu.VMEM((8, rows, width), bf16),
            pltpu.VMEM((7, rows, width), bf16),
            pltpu.VMEM((7, rows, width), bf16),
            pltpu.VMEM((7, rows, width), bf16),
            pltpu.VMEM((7, rows, width), bf16),
        ]
        + [dma((7,))] * 4 + [dma((8,))] * 2 + [dma((7,))] * 4 + [dma((8,))] * 2
        + [dma((2, 7))] * 4 + [dma((8,))] * 2,
        compiler_params=pltpu.CompilerParams(
            collective_id=0, has_side_effects=True, vmem_limit_bytes=63 << 20
        ),
    )(image_emb, text_emb, ids, logit_scale, bias)


def solution(mesh):
    placed = (P(("grp", "blk"), None), P(("grp", "blk"), None), P(("grp", "blk")), P(), P())
    return jax.shard_map(
        local,
        mesh=mesh,
        in_specs=placed,
        out_specs=(P(("grp", "blk"), None), P(("grp", "blk"), None)),
        check_vma=False,
    )
```

```python
import functools
import math

import jax
import jax.numpy as jnp
from jax import lax
from jax.experimental import pallas as pl
from jax.experimental.pallas import tpu as pltpu
from jax.sharding import PartitionSpec as P

epsilon = 1e-06
MESH = pl.DeviceIdType.MESH
NT = (((1,), (1,)), ((), ()))
TN = (((0,), (0,)), ((), ()))
LOG2E = math.log2(math.e)


def places():
    g, b = lax.axis_index("grp"), lax.axis_index("blk")
    z_lo, y = g // 4, g % 4
    x, z_hi, core = b // 4, (b // 2) % 2, b % 2
    z = z_hi * 2 + z_lo

    def device(x, y, z, core):
        return ((z % 2) * 4 + y, x * 4 + (z // 2) * 2 + core)

    toward_a, toward_b = 3 - 2 * core, 1 + 2 * core
    text = dict(
        a=device((x + toward_a) % 4, y, z, core),
        b=device((x + toward_b) % 4, y, z, core),
        z=device(x, y, (z // 2) * 2 + 1 - z % 2, core),
    )
    image = dict(
        a=device(x, (y + toward_a) % 4, z, core),
        b=device(x, (y + toward_b) % 4, z, core),
        z=device(x, y, 3 - z, core),
    )
    return text, image, device(x, y, z, 1 - core), core


def unit_rows(embedding):
    values = embedding.astype(jnp.float32)
    inverse = lax.rsqrt(jnp.sum(values * values, axis=1, keepdims=True) + epsilon)
    return values * inverse, inverse


def kernel(rows, width, image_in, text_in, ids_in, scale_in, bias_in, image_out, text_out,
           texts, images, text_ids, image_ids, text_col, image_col, image_row, factors, text_acc, text_far, image_acc,
           sib_out, sib_in, text_send, text_recv, image_send, image_recv,
           gt_s, gt_r, gi_s, gi_r, gs_s, gs_r, ht_s, ht_r, hi_s, hi_r, hs_s, hs_r,
           rt_s, rt_r, ri_s, ri_r, rs_s, rs_r):
    pair = 2 * rows
    text_at, image_at, sibling, core = places()
    near_a, near_b, far_a, far_b = 3 - core, 2 + core, 6 - core, 5 + core

    barrier = pltpu.get_barrier_semaphore()
    partners = [*text_at.values(), *image_at.values(), sibling]
    for partner in partners:
        pl.semaphore_signal(barrier, inc=1, device_id=partner, device_id_type=MESH)

    scale = jnp.exp(scale_in[0])
    scale2, offset2 = scale * LOG2E, bias_in[0] * LOG2E

    def text_rows(k):
        return pl.ds(pl.multiple_of(k * pair, 16), rows)

    def sib_rows(k):
        return pl.ds(pl.multiple_of(k * pair + rows, 16), rows)

    def image_rows(k):
        return pl.ds(pl.multiple_of(k * rows, 16), rows)

    texts[text_rows(0), :] = unit_rows(text_in[...])[0].astype(jnp.bfloat16)
    images[image_rows(0), :] = unit_rows(image_in[...])[0].astype(jnp.bfloat16)
    for held in (text_ids, image_ids):
        held[0] = jnp.zeros((8, 256), jnp.int32)
        held[0, :, 0:rows] = jnp.broadcast_to(ids_in[...], (8, rows))
    pl.semaphore_wait(barrier, len(partners))

    sent = []

    def remote(src, dst, send, recv, to):
        return pltpu.make_async_remote_copy(
            src_ref=src, dst_ref=dst, send_sem=send, recv_sem=recv, device_id=to, device_id_type=MESH
        )

    def launch(copy):
        copy.start()
        sent.append(copy)

    def push_text(m, k, k_there, to):
        launch(remote(texts.at[text_rows(k), :], texts.at[text_rows(k_there), :], gt_s.at[m], gt_r.at[m], to))

    def push_image(m, k, k_there, to):
        launch(remote(images.at[image_rows(k), :], images.at[image_rows(k_there), :], gi_s.at[m], gi_r.at[m], to))

    cuts = ((0, 96), (96, rows - 96))
    second = {1: 7, 3: 8, 6: 9}

    def text_cut(k, p):
        return pl.ds(pl.multiple_of(k * pair + cuts[p][0], 16), cuts[p][1])

    def image_cut(k, p):
        return pl.ds(pl.multiple_of(k * rows + cuts[p][0], 16), cuts[p][1])

    def push_cuts(m, k, k_there, to, some=(0, 1)):
        for p in some:
            i = m if p == 0 else second[m]
            launch(remote(texts.at[text_cut(k, p), :], texts.at[text_cut(k_there, p), :], gt_s.at[i], gt_r.at[i], text_at[to]))
            launch(remote(images.at[image_cut(k, p), :], images.at[image_cut(k_there, p), :], gi_s.at[i], gi_r.at[i], image_at[to]))

    def took_cut(m, k, p):
        i = m if p == 0 else second[m]
        took(texts.at[text_cut(k, p), :], gt_s.at[i], gt_r.at[i])
        took(images.at[image_cut(k, p), :], gi_s.at[i], gi_r.at[i])

    def push_sibling(k):
        launch(remote(texts.at[text_rows(k), :], texts.at[sib_rows(k), :], gs_s.at[k], gs_r.at[k], sibling))

    def took(place, send, recv):
        remote(place, place, send, recv, sibling).wait_recv()

    def took_text(m, k):
        took(texts.at[text_rows(k), :], gt_s.at[m], gt_r.at[m])

    def took_image(m, k):
        took(images.at[image_rows(k), :], gi_s.at[m], gi_r.at[m])

    def took_sibling(k):
        took(texts.at[sib_rows(k), :], gs_s.at[k], gs_r.at[k])

    def push_ids(m, k, k_there, to):
        launch(remote(text_ids.at[2 * k], text_ids.at[2 * k_there], ht_s.at[m], ht_r.at[m], text_at[to]))
        launch(remote(image_ids.at[k], image_ids.at[k_there], hi_s.at[m], hi_r.at[m], image_at[to]))

    def push_sibling_ids(k):
        launch(remote(text_ids.at[2 * k], text_ids.at[2 * k + 1], hs_s.at[k], hs_r.at[k], sibling))

    def took_ids(m, k):
        took(text_ids.at[2 * k], ht_s.at[m], ht_r.at[m])
        took(image_ids.at[k], hi_s.at[m], hi_r.at[m])
        push_sibling_ids(k)

    def column(ids):
        return jnp.transpose(ids)[:rows, 0:1]

    def text_columns(blocks):
        for k in blocks:
            text_col[k * pair:k * pair + rows, :] = column(text_ids[2 * k])
            text_col[k * pair + rows:(k + 1) * pair, :] = column(text_ids[2 * k + 1])

    def image_columns(blocks):
        for k in blocks:
            image_col[k * rows:(k + 1) * rows, :] = column(image_ids[k])

    def image_window(first, last):
        for w in range(first, last, 128):
            image_row[:, w:w + 128] = jnp.transpose(jnp.broadcast_to(image_col[w:w + 128, :], (128, 128)))[0:8, :]

    def factor_strip(start, count, first, last):
        some = pl.ds(start, count)
        products = lax.dot_general(texts[some, :], images[first:last, :], NT, preferred_element_type=jnp.float32)
        e = jnp.exp2(products * scale2 + offset2)
        match = text_col[some, :] == image_row[0:1, first:last]
        factors[some, first:last] = (jnp.where(match, -1.0, e) * pltpu.reciprocal(1.0 + e, approx=True)).astype(jnp.bfloat16)

    def factor_block(start, blocks, first, last):
        def strip(n, carry):
            factor_strip(pl.multiple_of(start + n * pair, 16), pair, first, last)
            return carry

        lax.fori_loop(0, blocks, strip, 0)

    near_texts, near_images = 5 * pair, 768

    def text_pairs(k):
        return pl.ds(pl.multiple_of(k * pair, 16), pair)

    def to_sibling(k, part):
        sib_out[k] = part.astype(jnp.bfloat16)
        launch(remote(sib_out.at[k], sib_in.at[k], rs_s.at[k], rs_r.at[k], sibling))

    def text_gradient(k):
        part = jnp.dot(factors[text_pairs(k), :], images[...], preferred_element_type=jnp.float32)
        text_acc[text_rows(k), :] = part[:rows]
        to_sibling(k, part[rows:])

    def far_text_gradient(k):
        part = jnp.dot(factors[text_pairs(k), :], images[...], preferred_element_type=jnp.float32)
        text_far[image_rows(k - 5), :] = part[:rows]
        to_sibling(k, part[rows:])

    def early_image_gradients(low, high):
        for first in range(low, high, 256):
            image_acc[first:first + 256, :] = lax.dot_general(
                factors[:near_texts, first:first + 256], texts[:near_texts, :], TN, preferred_element_type=jnp.float32)

    def image_gradient(first, last):
        image_acc[first:last, :] += lax.dot_general(
            factors[near_texts:, first:last], texts[near_texts:, :], TN, preferred_element_type=jnp.float32)

    def far_image_gradient(first, last):
        image_acc[first:last, :] = lax.dot_general(
            factors[:, first:last], texts[...], TN, preferred_element_type=jnp.float32)

    pieces = ((0, 96), (96, rows - 96))

    def piece_rows(start, p):
        return pl.ds(pl.multiple_of(start + pieces[p][0], 16), pieces[p][1])

    def wire(buffer, m, p):
        return buffer.at[m, pl.ds(*pieces[p]), :]

    def landed(buffer, sends, recvs, m, p):
        place = wire(buffer, m, p)
        remote(place, place, sends.at[p, m], recvs.at[p, m], sibling).wait_recv()
        return place[...].astype(jnp.float32)

    def text_sum(k, messages, p, far=False):
        if p == 0:
            remote(sib_in.at[k], sib_in.at[k], rs_s.at[k], rs_r.at[k], sibling).wait_recv()
        held = text_far[piece_rows((k - 5) * rows, p), :] if far else text_acc[piece_rows(k * pair, p), :]
        total = held + wire(sib_in, k, p)[...].astype(jnp.float32)
        for m in messages:
            total = total + landed(text_recv, rt_s, rt_r, m, p)
        return total

    def image_sum(k, messages, p):
        total = image_acc[piece_rows(k * rows, p), :]
        for m in messages:
            total = total + landed(image_recv, ri_s, ri_r, m, p)
        return total

    def text_hop(k, messages, m, to, far=False, some=(0, 1)):
        for p in some:
            wire(text_send, m, p)[...] = text_sum(k, messages, p, far).astype(jnp.bfloat16)
            launch(remote(wire(text_send, m, p), wire(text_recv, m, p), rt_s.at[p, m], rt_r.at[p, m], text_at[to]))

    def image_hop(k, messages, m, to, some=(0, 1)):
        for p in some:
            wire(image_send, m, p)[...] = image_sum(k, messages, p).astype(jnp.bfloat16)
            launch(remote(wire(image_send, m, p), wire(image_recv, m, p), ri_s.at[p, m], ri_r.at[p, m], image_at[to]))

    def finish(embedding, gradient):
        scaled, inverse = unit_rows(embedding)
        gradient = gradient * scale
        along = jnp.sum(scaled * gradient, axis=1, keepdims=True)
        return ((gradient - scaled * along) * inverse).astype(jnp.bfloat16)

    def text_done(p):
        some = pl.ds(*pieces[p])
        text_out[some, :] = finish(text_in[some, :], text_sum(0, (5, 6, 4), p))

    def image_done(p):
        some = pl.ds(*pieces[p])
        image_out[some, :] = finish(image_in[some, :], image_sum(0, (5, 6, 4), p))

    own_to = ((1, near_a, "b"), (0, near_b, "a"), (2, 1, "z"))
    for m, k_there, to in own_to:
        push_ids(m, 0, k_there, to)
    push_sibling_ids(0)
    push_cuts(1, 0, near_a, "b")
    for m, k_there, to in own_to[1:]:
        push_text(m, 0, k_there, text_at[to])
        push_image(m, 0, k_there, image_at[to])
    push_sibling(0)
    took_ids(1, near_a)
    push_ids(3, near_a, 4, "b")
    took_ids(2, 1)
    push_ids(4, 1, far_b, "a")
    push_ids(5, 1, far_a, "b")
    took_ids(0, near_b)
    for k in (0, near_a, 1, near_b):
        took(text_ids.at[2 * k + 1], hs_s.at[k], hs_r.at[k])
    text_columns([0, 1, 2, 3])
    image_columns([0, 1, 2, 3])
    image_window(0, 512)

    took_cut(1, near_a, 0)
    push_cuts(3, near_a, 4, "b", (0,))
    took_cut(1, near_a, 1)
    push_cuts(3, near_a, 4, "b", (1,))
    took_text(2, 1)
    push_text(4, 1, far_b, text_at["a"])
    push_text(5, 1, far_a, text_at["b"])
    took_image(2, 1)
    push_image(4, 1, far_b, image_at["a"])
    push_image(5, 1, far_a, image_at["b"])
    push_sibling(near_a)
    push_sibling(1)
    took_text(0, near_b)
    push_sibling(near_b)
    took_image(0, near_b)
    took_ids(3, 4)
    push_ids(6, 4, 7, "z")
    took_cut(3, 4, 0)
    push_cuts(6, 4, 7, "z", (0,))
    for k in (0, near_a, 1, near_b):
        took_sibling(k)
    factor_block(0, 4, 0, 512)

    took_cut(3, 4, 1)
    push_cuts(6, 4, 7, "z", (1,))
    push_sibling(4)
    took_ids(4, far_b)
    took_ids(5, far_a)
    took_ids(6, 7)
    for k in (4, far_b, far_a, 7):
        took(text_ids.at[2 * k + 1], hs_s.at[k], hs_r.at[k])
    text_columns([4, 5, 6, 7])
    image_columns([4, 5, 6, 7])
    image_window(512, 1408)
    took_sibling(4)
    factor_block(0, 4, 512, 768)
    factor_block(4 * pair, 1, 0, 768)
    early_image_gradients(0, 512)

    took_text(4, far_b)
    push_sibling(far_b)
    took_text(5, far_a)
    push_sibling(far_a)
    took_cut(6, 7, 0)
    took_cut(6, 7, 1)
    push_sibling(7)
    took_image(4, far_b)
    took_image(5, far_a)
    early_image_gradients(512, 768)
    for k in (far_b, far_a, 7):
        took_sibling(k)

    factor_block(7 * pair, 1, 0, 1408)
    far_text_gradient(7)
    factor_block(5 * pair, 1, 0, 1408)
    text_hop(7, (), 0, "z", far=True)
    factor_block(6 * pair, 1, 0, 1408)
    image_gradient(256, 768)
    image_hop(near_b, (), 5, "b")
    far_text_gradient(5)
    far_text_gradient(6)
    factor_block(0, 2, 768, 1408)
    text_hop(far_a, (), 2, "a", far=True)
    text_hop(far_b, (), 3, "b", far=True)
    factor_block(2 * pair, 3, 768, 1408)
    far_image_gradient(1152, 1408)
    image_hop(7, (), 0, "z")
    far_image_gradient(768, 1152)
    image_hop(far_a, (), 2, "a")
    image_hop(far_b, (), 3, "b")
    text_gradient(4)
    text_gradient(2)
    text_hop(4, (0,), 1, "a")
    text_gradient(3)
    text_hop(near_b, (), 5, "b")
    image_hop(4, (0,), 1, "a", (0,))
    text_gradient(1)
    image_hop(4, (0,), 1, "a", (1,))
    image_gradient(0, 256)
    text_hop(1, (2, 3), 6, "z")
    image_hop(1, (2, 3), 6, "z", (0,))
    text_gradient(0)
    image_hop(1, (2, 3), 6, "z", (1,))
    image_hop(near_a, (1,), 4, "a", (0,))
    text_hop(near_a, (1,), 4, "a")
    image_hop(near_a, (1,), 4, "a", (1,))
    text_done(0)
    text_done(1)
    image_done(0)
    image_done(1)
    for copy in sent:
        copy.wait_send()


def local(image_emb, text_emb, pair_ids, logit_scale, bias):
    rows, width = image_emb.shape
    ids = pair_ids.reshape(1, rows)
    bf16, f32, i32 = jnp.bfloat16, jnp.float32, jnp.int32
    vmem, smem = pl.BlockSpec(memory_space=pltpu.VMEM), pl.BlockSpec(memory_space=pltpu.SMEM)
    dma = pltpu.SemaphoreType.DMA
    return pl.pallas_call(
        functools.partial(kernel, rows, width),
        out_shape=[jax.ShapeDtypeStruct((rows, width), bf16)] * 2,
        in_specs=[vmem, vmem, vmem, smem, smem],
        out_specs=[vmem, vmem],
        scratch_shapes=[
            pltpu.VMEM((16 * rows, width), bf16),
            pltpu.VMEM((8 * rows, width), bf16),
            pltpu.VMEM((16, 8, 256), i32),
            pltpu.VMEM((8, 8, 256), i32),
            pltpu.VMEM((16 * rows, 1), i32),
            pltpu.VMEM((8 * rows, 1), i32),
            pltpu.VMEM((8, 8 * rows), i32),
            pltpu.VMEM((16 * rows, 8 * rows), bf16),
            pltpu.VMEM((10 * rows, width), f32),
            pltpu.VMEM((3 * rows, width), f32),
            pltpu.VMEM((8 * rows, width), f32),
            pltpu.VMEM((8, rows, width), bf16),
            pltpu.VMEM((8, rows, width), bf16),
            pltpu.VMEM((7, rows, width), bf16),
            pltpu.VMEM((7, rows, width), bf16),
            pltpu.VMEM((7, rows, width), bf16),
            pltpu.VMEM((7, rows, width), bf16),
        ]
        + [dma((10,))] * 4 + [dma((8,))] * 2 + [dma((7,))] * 4 + [dma((8,))] * 2
        + [dma((2, 7))] * 4 + [dma((8,))] * 2,
        compiler_params=pltpu.CompilerParams(
            collective_id=0, has_side_effects=True, vmem_limit_bytes=63 << 20
        ),
    )(image_emb, text_emb, ids, logit_scale, bias)


def solution(mesh):
    placed = (P(("grp", "blk"), None), P(("grp", "blk"), None), P(("grp", "blk")), P(), P())
    return jax.shard_map(
        local,
        mesh=mesh,
        in_specs=placed,
        out_specs=(P(("grp", "blk"), None), P(("grp", "blk"), None)),
        check_vma=False,
    )
```
